512 devices in a mesh: batch: 2 (over core), token: 32 (over x, z), hidden: 8 (over y).
Axes of the slice: x: 4, y: 8, z: 8, core: 2. Of those that a mesh axis runs over, the one named last changes fastest.
Arguments:
- hist_len: int32 [512], replicated, may hold values from 32 to 512, as said below
- queries: bfloat16 [32, 1536], P(None, 'token'), may hold values from -4 to 4
- history_keys: bfloat16 [1536, 1536, 128], P(('batch', 'hidden'), 'token'), may hold values from -192 to 192
- cached_history_values: bfloat16 [1536, 1536, 128], P(('batch', 'hidden'), 'token'), may hold values from -6 to 6
- gain_mix: float32 [1536], replicated, may hold values from 0.25 to 1.75
- w_up: bfloat16 [32, 1536, 3072], P('token', None, 'hidden'), may hold values from -0.15625 to 0.15625
- w_down: bfloat16 [32, 3072, 1536], P('token', 'hidden'), may hold values from -0.109375 to 0.109375
- gain_out: float32 [1536], replicated, may hold values from 0.25 to 1.75
Outputs:
- mixer_out: bfloat16 [512, 32, 1536], P(('batch', 'hidden'), 'token')
The draws below stay inside these ranges and needn't reach their ends.
Inputs may be any that keep to these rules, and one draw needn't show every extreme that they name: `hist_len`: along batch+hidden, the requests of each index need between 32 and 96 slots, indices 2i and 2i + 1 need 4 * 32 slots together, and some index needs exactly 96; within an index, requests 2j and 2j + 1 need from 2 to 6 slots together.
All inputs are finite; a program needn't handle non-finite values.
Results may differ from the reference program's by a relative error of at most 0.015.
Values may be sent and summed in bfloat16 or wider, within the bound.
A program may use at most 64 MiB of HBM per device.

```python
import jax
import jax.numpy as jnp
from jax import lax

TOKEN_COUNT = 32
MODEL_WIDTH = 1536
FF = 3072
BLOCK_POSITIONS = 128
REQ_DEV = 32
SLOTS = 96
REQUESTS = 512
SLOT_TOTAL = 1536
N_BATCH = 2
N_HIDDEN = 8


def make_queries(seed_key):
    return jnp.clip(jax.random.normal(seed_key, (TOKEN_COUNT, MODEL_WIDTH), jnp.float32), -4.0, 4.0)


def draw_queries(key, part):
    return make_queries(jax.random.fold_in(key, 17)).astype(jnp.bfloat16)


def draw_history_keys(key, part):
    drawn_version = jnp.clip(jax.random.normal(jax.random.fold_in(key, 23), (SLOT_TOTAL, MODEL_WIDTH, BLOCK_POSITIONS), jnp.float32), -6.0, 6.0)
    return drawn_version.astype(jnp.bfloat16)


def draw_hist_len(key, part):
    group_size = N_BATCH * N_HIDDEN
    pair_count = group_size // 2
    heavy = jax.random.randint(jax.random.fold_in(key, 41), (pair_count,), 0, 5)
    forced = jax.random.randint(jax.random.fold_in(key, 43), (), 0, pair_count)
    heavy = jnp.where(jnp.arange(pair_count) == forced, 4, heavy)
    level = jnp.stack([heavy, 4 - heavy], axis=1).reshape(group_size)
    lowest = jnp.maximum(level - 3, 0)
    highest = jnp.minimum(level, 3)
    leading_part = jax.random.randint(jax.random.fold_in(key, 47), (group_size, REQ_DEV // 2), lowest[:, None], highest[:, None] + 1)
    extra = jnp.stack([leading_part, level[:, None] - leading_part], axis=2).reshape(group_size, REQ_DEV)
    tail_rows = jax.random.randint(jax.random.fold_in(key, 53), (group_size, REQ_DEV), BLOCK_POSITIONS // 4, BLOCK_POSITIONS + 1)
    return (extra * BLOCK_POSITIONS + tail_rows).reshape(group_size * REQ_DEV).astype(jnp.int32)


def block_levels(key, shape, shards, low, high):
    level, own = 1.0, jax.random.fold_in(key, 6)
    for dim, parts in shards:
        draws = jnp.exp(jax.random.uniform(jax.random.fold_in(own, dim), (parts,), jnp.float32, low / len(shards), high / len(shards)))
        level = level * jnp.repeat(draws, shape[dim] // parts).reshape([-1 if axis == dim else 1 for axis in range(len(shape))])
    return level


def normal_values(own_key, shape, spread, limit, shards=(), held_as=jnp.bfloat16):
    entries = spread * jax.random.normal(own_key, shape, jnp.float32)
    if shards:
        entries = entries * block_levels(own_key, shape, shards, -0.22, 0.18)
    return jnp.clip(entries, -limit, limit).astype(held_as)


def setup_inputs(seed: int = 0) -> dict:
    arg_keys = jax.random.split(jax.random.key(seed), 9)
    return {
        "hist_len": draw_hist_len(jax.random.fold_in(arg_keys[8], 71), 0),
        "queries": draw_queries(jax.random.fold_in(arg_keys[8], 71), 0),
        "history_keys": draw_history_keys(jax.random.fold_in(arg_keys[8], 71), 0),
        "cached_history_values": normal_values(arg_keys[3], (SLOT_TOTAL, MODEL_WIDTH, BLOCK_POSITIONS), 1.0, 6.0, ((0, 16), (1, 32))),
        "gain_mix": jnp.clip(1.0 + 0.15 * jax.random.normal(arg_keys[4], (MODEL_WIDTH,), jnp.float32), 0.25, 1.75),
        "w_up": normal_values(arg_keys[5], (TOKEN_COUNT, MODEL_WIDTH, FF), MODEL_WIDTH ** -0.5, 0.15625, ((0, 32), (2, 8))),
        "w_down": normal_values(arg_keys[6], (TOKEN_COUNT, FF, MODEL_WIDTH), FF ** -0.5, 0.109375, ((0, 32), (1, 8))),
        "gain_out": jnp.clip(1.0 + 0.15 * jax.random.normal(arg_keys[7], (MODEL_WIDTH,), jnp.float32), 0.25, 1.75),
    }


EPSILON = 1e-05
NEGATIVE_FILL = -1e+30

def slot_layout(lengths, slot_count, block_rows):
    request_count = lengths.shape[0]
    blocks = ((lengths + block_rows - 1) // block_rows).astype(jnp.int32)
    block_ends = jnp.cumsum(blocks).astype(jnp.int32)
    block_starts = block_ends - blocks
    slot_index = jnp.arange(slot_count, dtype=jnp.int32)
    owners = lax.optimization_barrier(jnp.sum((block_ends[None, :] <= slot_index[:, None]).astype(jnp.int32), axis=1)).astype(jnp.int32)
    onehot = owners[:, None] == jnp.arange(request_count, dtype=jnp.int32)[None, :]
    start_of = lax.optimization_barrier(jnp.sum(jnp.where(onehot, block_starts[None, :], 0), axis=1)).astype(jnp.int32)
    length_of = lax.optimization_barrier(jnp.sum(jnp.where(onehot, lengths[None, :], 0), axis=1)).astype(jnp.int32)
    valid_rows = jnp.clip(length_of - (slot_index - start_of) * block_rows, 0, block_rows)
    return (onehot, valid_rows.astype(jnp.int32))

def block_partials(query_heads, slot_keys, slot_values, valid_rows, score_scale):
    scores = jnp.einsum('qhs,nhsp->nqhp', query_heads.astype(jnp.float32), slot_keys.astype(jnp.float32), precision=lax.Precision.HIGHEST) * score_scale
    position = jnp.arange(slot_keys.shape[-1], dtype=jnp.int32)
    in_range = position[None, None, None, :] < valid_rows[:, None, None, None]
    scores = jnp.where(in_range, scores, NEGATIVE_FILL)
    maxima = lax.optimization_barrier(jnp.max(scores, axis=-1))
    softmax_terms = jnp.where(in_range, jnp.exp(scores - maxima[..., None]), 0.0)
    totals = lax.optimization_barrier(jnp.sum(softmax_terms, axis=-1))
    rounded_terms = softmax_terms.astype(jnp.bfloat16).astype(jnp.float32)
    weighted = jnp.einsum('nqhp,nhsp->nqhs', rounded_terms, slot_values.astype(jnp.float32), precision=lax.Precision.HIGHEST)
    return (maxima, totals, weighted)

def combine_blocks(maxima, totals, weighted, onehot):
    owned = onehot.astype(jnp.float32)
    is_live = lax.optimization_barrier(jnp.sum(owned, axis=1)) > 0.5
    masked_max = jnp.where(onehot[:, :, None, None], maxima[:, None, :, :], NEGATIVE_FILL)
    request_max = lax.optimization_barrier(jnp.max(masked_max, axis=0))
    owner_max = jnp.einsum('nr,rqh->nqh', owned, request_max, precision=lax.Precision.HIGHEST)
    factor = jnp.exp(jnp.where(is_live[:, None, None], maxima - owner_max, NEGATIVE_FILL))
    denominator = jnp.einsum('nr,nqh->rqh', owned, factor * totals, precision=lax.Precision.HIGHEST)
    numerator = jnp.einsum('nr,nqhs->rqhs', owned, factor[..., None] * weighted, precision=lax.Precision.HIGHEST)
    return (numerator / denominator[..., None]).astype(jnp.bfloat16)

def layer_norm(summand):
    average = lax.optimization_barrier(jnp.mean(summand, axis=-1, keepdims=True))
    centred = summand - average
    variance = lax.optimization_barrier(jnp.mean(centred * centred, axis=-1, keepdims=True))
    return centred * lax.rsqrt(variance + EPSILON)

def reference(hist_len, queries, history_keys, cached_history_values, gain_mix, w_up, w_down, gain_out):
    head_size = MODEL_WIDTH // TOKEN_COUNT
    group_count = hist_len.shape[0] // REQ_DEV
    query_heads = queries.reshape(TOKEN_COUNT, TOKEN_COUNT, head_size)
    score_scale = head_size ** (-0.5)

    def one_group(group_id):
        lengths = lax.dynamic_slice_in_dim(hist_len, group_id * REQ_DEV, REQ_DEV)
        slot_keys = lax.dynamic_slice_in_dim(history_keys, group_id * SLOTS, SLOTS).reshape(SLOTS, TOKEN_COUNT, head_size, BLOCK_POSITIONS)
        slot_values = lax.dynamic_slice_in_dim(cached_history_values, group_id * SLOTS, SLOTS).reshape(SLOTS, TOKEN_COUNT, head_size, BLOCK_POSITIONS)
        onehot, valid_rows = slot_layout(lengths, SLOTS, BLOCK_POSITIONS)
        maxima, totals, weighted = block_partials(query_heads, slot_keys, slot_values, valid_rows, score_scale)
        return combine_blocks(maxima, totals, weighted, onehot)
    attended = lax.map(one_group, jnp.arange(group_count, dtype=jnp.int32))
    attended = attended.reshape(REQUESTS, TOKEN_COUNT, TOKEN_COUNT, head_size)
    mixed_rows = jnp.transpose(attended, (0, 2, 1, 3)).reshape(REQUESTS, TOKEN_COUNT, MODEL_WIDTH)
    unmixed = attended.reshape(REQUESTS, TOKEN_COUNT, MODEL_WIDTH)
    joined = mixed_rows.astype(jnp.float32) + unmixed.astype(jnp.float32)
    normed = (layer_norm(joined) * gain_mix).astype(jnp.bfloat16)

    def token_ffn(operands):
        token_rows, up_weight, down_weight = operands
        lifted = jnp.dot(token_rows, up_weight, preferred_element_type=jnp.float32)
        activated = jax.nn.gelu(lifted, approximate=False).astype(jnp.bfloat16)
        return jnp.dot(activated, down_weight, preferred_element_type=jnp.float32)
    ffn_out = lax.map(token_ffn, (jnp.transpose(normed, (1, 0, 2)), w_up, w_down))
    ffn_out = jnp.transpose(ffn_out, (1, 0, 2))
    return (layer_norm(ffn_out + normed.astype(jnp.float32)) * gain_out).astype(jnp.bfloat16)
```

```python
import functools
import math

import jax
import jax.numpy as jnp
from jax import lax
from jax.experimental import pallas as pl
from jax.experimental.pallas import tpu as pltpu
from jax.sharding import PartitionSpec as P

TOKENS = 32
WIDTH = 1536
HEAD = 48
POS = 128
REQ_DEV = 32
SLOTS = 96
RING = 8
HALVES = 2
ROWS = REQ_DEV // HALVES
PAIR_SLOTS = 6
PAIRS = ROWS // 2
UNROLL = 4
MID = WIDTH // 2
FILL = -1e30
EPSILON = 1e-5
MESH = pl.DeviceIdType.MESH


def layer_norm(x):
    mean = jnp.sum(x, axis=-1, keepdims=True) * (1.0 / WIDTH)
    c = x - mean
    var = jnp.sum(c * c, axis=-1, keepdims=True) * (1.0 / WIDTH)
    return c * lax.rsqrt(var + EPSILON)


def kernel(
    len_ref, q_ref, gain_ref, k_hbm, v_hbm, up_hbm, down_hbm,
    out_ref,
    k_ref, v_ref, up_ref, down_ref, att, tiles, others, rows, part, out_buf, in_buf,
    load_sem, a2a_send, a2a_recv, ag_send, ag_recv, rs_send, rs_recv,
):
    me = lax.axis_index("token")
    y = lax.axis_index("hidden")
    group = lax.axis_index("batch") * RING + y
    above, below = lax.rem(y + 1, RING), lax.rem(y + RING - 1, RING)

    loads = [
        pltpu.make_async_copy(k_hbm, k_ref, load_sem.at[0]),
        pltpu.make_async_copy(v_hbm, v_ref, load_sem.at[1]),
        pltpu.make_async_copy(up_hbm.at[0], up_ref, load_sem.at[2]),
        pltpu.make_async_copy(down_hbm.at[0], down_ref, load_sem.at[3]),
    ]
    for load in loads:
        load.start()

    barrier = pltpu.get_barrier_semaphore()

    def greet(i, c):
        pl.semaphore_signal(
            barrier, inc=1, device_id={"token": lax.rem(me + i, TOKENS)}, device_id_type=MESH
        )
        return c

    lax.fori_loop(1, TOKENS, greet, 0)
    for near in (above, below):
        pl.semaphore_signal(barrier, inc=1, device_id={"hidden": near}, device_id_type=MESH)

    att[...] = jnp.zeros_like(att)
    position = lax.broadcasted_iota(jnp.int32, (1, PAIR_SLOTS * POS), 1)
    scale = HEAD ** -0.5
    loads[0].wait()
    loads[1].wait()

    def attend_pair(pair, start, half):
        request = group * REQ_DEV + half * ROWS + pair * 2
        len_a, len_b = len_ref[request], len_ref[request + 1]
        used_a = lax.shift_right_logical(len_a + (POS - 1), 7)
        used_b = lax.shift_right_logical(len_b + (POS - 1), 7)
        slot = [jnp.minimum(start + i, SLOTS - 1) for i in range(PAIR_SLOTS)]
        keys = jnp.concatenate([k_ref[s] for s in slot], axis=1)
        values = jnp.concatenate([v_ref[s] for s in slot], axis=1)
        score = jnp.dot(q_ref[...], keys, preferred_element_type=jnp.float32) * scale
        edge = used_a * POS
        of_a = position < edge
        in_a = position < len_a
        in_b = jnp.logical_and(position >= edge, position < edge + len_b)
        max_a = jnp.max(jnp.where(in_a, score, FILL), axis=1, keepdims=True)
        max_b = jnp.max(jnp.where(in_b, score, FILL), axis=1, keepdims=True)
        term = jnp.exp(score - jnp.where(of_a, max_a, max_b))
        term_a = jnp.where(in_a, term, 0.0)
        term_b = jnp.where(in_b, term, 0.0)
        both = jnp.concatenate([term_a, term_b], axis=0)
        total = jnp.sum(both, axis=1, keepdims=True)
        acc = lax.dot_general(
            both.astype(jnp.bfloat16), values, (((1,), (1,)), ((), ())),
            preferred_element_type=jnp.float32,
        )
        row = pl.multiple_of(pair * (2 * TOKENS), 2 * TOKENS)
        att[pl.ds(row, 2 * TOKENS), 0:HEAD] = acc / total
        return start + used_a + used_b

    def attend(half, start):
        def step(i, start):
            for u in range(UNROLL):
                start = attend_pair(i * UNROLL + u, start, half)
            return start

        start = lax.fori_loop(0, PAIRS // UNROLL, step, start)
        for q in range(TOKENS):
            tiles[half, q] = att[pl.ds(q, ROWS, stride=TOKENS), :].astype(jnp.bfloat16)
        others[half, me] = tiles[half, me]
        return start

    def exchange(half):
        def send(i, c):
            to = lax.rem(me + i, TOKENS)
            pltpu.make_async_remote_copy(
                src_ref=tiles.at[half, to],
                dst_ref=others.at[half, me],
                send_sem=a2a_send.at[half],
                recv_sem=a2a_recv.at[half],
                device_id={"token": to},
                device_id_type=MESH,
            ).start()
            return c

        lax.fori_loop(1, TOKENS, send, 0)

    def all_tiles(ref, half, sem):
        some = ref.at[half, pl.ds(0, TOKENS - 1)]
        return pltpu.make_async_copy(some, some, sem.at[half])

    lane = lax.broadcasted_iota(jnp.int32, (ROWS, 128), 1)

    def mix(half):
        all_tiles(others, half, a2a_recv).wait()
        out = [None] * (WIDTH // 128)
        for j in range(TOKENS):
            x = tiles[half, j].astype(jnp.float32) + others[half, j].astype(jnp.float32)
            first = j * HEAD
            shift = first % 128
            if shift:
                x = pltpu.roll(x, shift, 1)
            t = first // 128
            if shift + HEAD > 128:
                out[t] = jnp.where(lane >= shift, x, out[t])
                out[t + 1] = x
            else:
                out[t] = x if out[t] is None else jnp.where(lane >= shift, x, out[t])
        normed = layer_norm(jnp.concatenate(out, axis=1)) * gain_ref[0:1, :]
        rows[half, y] = normed.astype(jnp.bfloat16)

    LOW, HIGH, ALL = pl.ds(0, MID), pl.ds(MID, MID), pl.ds(0, WIDTH)

    def gather(half, way, hop):
        to = (above, below)[way]
        back = hop - 1
        source = lax.rem(y + (RING - back if way == 0 else back), RING)
        cols = ALL if hop < 4 else (LOW, HIGH)[way]
        block = rows.at[half, source, :, cols]
        return pltpu.make_async_remote_copy(
            src_ref=block, dst_ref=block,
            send_sem=ag_send.at[half, way, hop - 1], recv_sem=ag_recv.at[half, way, hop - 1],
            device_id={"hidden": to}, device_id_type=MESH,
        )

    def arrived(half, way, hop):
        source = lax.rem(y + (RING - hop if way == 0 else hop), RING)
        cols = ALL if hop < 4 else (LOW, HIGH)[way]
        block = rows.at[half, source, :, cols]
        return pltpu.make_async_remote_copy(
            src_ref=block, dst_ref=block,
            send_sem=ag_send.at[half, way, hop - 1], recv_sem=ag_recv.at[half, way, hop - 1],
            device_id={"hidden": (below, above)[way]}, device_id_type=MESH,
        )

    def forward(half, hop):
        for way in range(2):
            arrived(half, way, hop).wait_recv()
            if hop < 4:
                gather(half, way, hop + 1).start()

    ORDER = [0, RING - 1, 1, RING - 2, 2, RING - 3, 3, 4]

    def ffn(half, first, last):
        x = jnp.concatenate(
            [rows[half, lax.rem(y + ORDER[i], RING)] for i in range(first, last)], axis=0
        )
        up = jnp.dot(x, up_ref[...], preferred_element_type=jnp.float32)
        act = (0.5 * up * (1.0 + lax.erf(up * math.sqrt(0.5)))).astype(jnp.bfloat16)
        down = jnp.dot(act, down_ref[...], preferred_element_type=jnp.float32)
        part[half, first:last] = down.reshape(last - first, ROWS, WIDTH)

    def sums(half, way, step):
        cols = ALL if step else (LOW, HIGH)[way]
        return pltpu.make_async_remote_copy(
            src_ref=out_buf.at[half, way, step, :, cols],
            dst_ref=in_buf.at[half, way, step, :, cols],
            send_sem=rs_send.at[half, way, step], recv_sem=rs_recv.at[half, way, step],
            device_id={"hidden": (below, above)[way]}, device_id_type=MESH,
        )

    def scatter(half, step):
        d = 4 - step
        for way in range(2):
            if step == 0:
                cols = (slice(0, MID), slice(MID, WIDTH))[way]
                out_buf[half, way, 0, :, cols] = part[half, 7, :, cols].astype(jnp.bfloat16)
            else:
                sums(half, way, step - 1).wait_recv()
                own = 2 * d - 1 + way
                for got, cols in ((0, slice(0, MID)), (1, slice(MID, WIDTH))):
                    x = part[half, own, :, cols]
                    if step > 1 or got == way:
                        x = x + in_buf[half, way, step - 1, :, cols].astype(jnp.float32)
                    out_buf[half, way, step, :, cols] = x.astype(jnp.bfloat16)
            sums(half, way, step).start()

    def finish(half):
        total = part[half, 0] + rows[half, y].astype(jnp.float32)
        for way in range(2):
            sums(half, way, 3).wait_recv()
            total = total + in_buf[half, way, 3].astype(jnp.float32)
        out_ref[half * ROWS : (half + 1) * ROWS, :] = (
            layer_norm(total) * gain_ref[1:2, :]
        ).astype(jnp.bfloat16)

    start = attend(0, 0)
    pl.semaphore_wait(barrier, TOKENS + 1)
    exchange(0)
    attend(1, start)
    exchange(1)
    for half in range(HALVES):
        mix(half)
        for way in range(2):
            gather(half, way, 1).start()
    forward(0, 1)
    forward(1, 1)
    loads[2].wait()
    loads[3].wait()
    forward(0, 2)
    ffn(0, 0, 5)
    forward(1, 2)
    forward(0, 3)
    ffn(1, 0, 5)
    forward(1, 3)
    forward(0, 4)
    ffn(0, 5, 8)
    scatter(0, 0)
    forward(1, 4)
    ffn(1, 5, 8)
    scatter(1, 0)
    for step in range(1, 4):
        scatter(0, step)
        scatter(1, step)
    finish(0)
    finish(1)

    for half in range(HALVES):
        all_tiles(tiles, half, a2a_send).wait()
        for way in range(2):
            for hop in range(1, 5):
                gather(half, way, hop).wait_send()
            for step in range(4):
                sums(half, way, step).wait_send()


def local(hist_len, queries, history_keys, cached_history_values, gain_mix, w_up, w_down, gain_out):
    vmem = pl.BlockSpec(memory_space=pltpu.VMEM)
    hbm = pl.BlockSpec(memory_space=pl.ANY)
    bf16, f32 = jnp.bfloat16, jnp.float32
    dma = pltpu.SemaphoreType.DMA
    out = pl.pallas_call(
        kernel,
        out_shape=jax.ShapeDtypeStruct((REQ_DEV, WIDTH), bf16),
        in_specs=[pl.BlockSpec(memory_space=pltpu.SMEM), vmem, vmem, hbm, hbm, hbm, hbm],
        out_specs=vmem,
        scratch_shapes=[
            pltpu.VMEM((SLOTS, HEAD, POS), bf16),
            pltpu.VMEM((SLOTS, HEAD, POS), bf16),
            pltpu.VMEM(w_up.shape[1:], bf16),
            pltpu.VMEM(w_down.shape[1:], bf16),
            pltpu.VMEM((ROWS * TOKENS, 128), f32),
            pltpu.VMEM((HALVES, TOKENS, ROWS, 128), bf16),
            pltpu.VMEM((HALVES, TOKENS, ROWS, 128), bf16),
            pltpu.VMEM((HALVES, RING, ROWS, WIDTH), bf16),
            pltpu.VMEM((HALVES, RING, ROWS, WIDTH), f32),
            pltpu.VMEM((HALVES, 2, 4, ROWS, WIDTH), bf16),
            pltpu.VMEM((HALVES, 2, 4, ROWS, WIDTH), bf16),
            dma((4,)),
            dma((HALVES,)),
            dma((HALVES,)),
            dma((HALVES, 2, 4)),
            dma((HALVES, 2, 4)),
            dma((HALVES, 2, 4)),
            dma((HALVES, 2, 4)),
        ],
        compiler_params=pltpu.CompilerParams(
            collective_id=0, has_side_effects=True, vmem_limit_bytes=60 * 2**20
        ),
        cost_estimate=pl.CostEstimate(
            flops=700_000_000, bytes_accessed=5_000_000, transcendentals=500_000
        ),
    )(
        hist_len, queries, jnp.stack([gain_mix, gain_out]),
        history_keys, cached_history_values, w_up, w_down,
    )
    return out.reshape(REQ_DEV, 1, WIDTH)


def solution(mesh):
    return jax.shard_map(
        local,
        mesh=mesh,
        in_specs=(
            P(),
            P(None, "token"),
            P(("batch", "hidden"), "token", None),
            P(("batch", "hidden"), "token", None),
            P(),
            P("token", None, "hidden"),
            P("token", "hidden", None),
            P(),
        ),
        out_specs=P(("batch", "hidden"), "token", None),
        check_vma=False,
    )
```

```python
import functools
import math

import jax
import jax.numpy as jnp
from jax import lax
from jax.experimental import pallas as pl
from jax.experimental.pallas import tpu as pltpu
from jax.sharding import PartitionSpec as P

TOKENS = 32
WIDTH = 1536
HEAD = 48
POS = 128
REQ_DEV = 32
SLOTS = 96
RING = 8
HALVES = 2
ROWS = REQ_DEV // HALVES
PAIR_SLOTS = 6
PAIRS = REQ_DEV // 2
UNROLL = 4
MID = WIDTH // 2
FILL = -1e30
EPSILON = 1e-5
MESH = pl.DeviceIdType.MESH
SIDE = 8
OFFSETS = sorted(
    ((dx, dz) for dx in range(TOKENS // SIDE) for dz in range(SIDE) if dx or dz),
    key=lambda o: (-min(o[0], TOKENS // SIDE - o[0]) - min(o[1], SIDE - o[1]), o),
)


def layer_norm(x):
    mean = jnp.sum(x, axis=-1, keepdims=True) * (1.0 / WIDTH)
    c = x - mean
    var = jnp.sum(c * c, axis=-1, keepdims=True) * (1.0 / WIDTH)
    return c * lax.rsqrt(var + EPSILON)


def kernel(
    len_ref, q_ref, mix_gain, out_gain, k_hbm, v_hbm, up_hbm, down_hbm,
    out_ref,
    k_ref, v_ref, up_ref, down_ref, att, tiles, others, rows, part, out_buf, in_buf,
    load_sem, a2a_send, a2a_recv, ag_send, ag_recv, rs_send, rs_recv,
):
    me = lax.axis_index("token")
    y = lax.axis_index("hidden")
    group = lax.axis_index("batch") * RING + y

    def at(distance):
        return lax.rem(y + RING + distance, RING)


    def peer(offset):
        x, z = me // SIDE, lax.rem(me, SIDE)
        return lax.rem(x + offset[0], TOKENS // SIDE) * SIDE + lax.rem(z + offset[1], SIDE)

    barrier = pltpu.get_barrier_semaphore()
    for offset in OFFSETS:
        pl.semaphore_signal(
            barrier, inc=1, device_id={"token": peer(offset)}, device_id_type=MESH
        )
    for step in (2, -2, 1, -1):
        pl.semaphore_signal(
            barrier, inc=1, device_id={"hidden": at(step)}, device_id_type=MESH
        )

    loads = [
        pltpu.make_async_copy(k_hbm, k_ref, load_sem.at[0]),
        pltpu.make_async_copy(v_hbm, v_ref, load_sem.at[1]),
        pltpu.make_async_copy(up_hbm.at[0], up_ref, load_sem.at[2]),
        pltpu.make_async_copy(down_hbm.at[0], down_ref, load_sem.at[3]),
    ]
    for load in loads:
        load.start()

    att[...] = jnp.zeros_like(att)
    position = lax.broadcasted_iota(jnp.int32, (1, PAIR_SLOTS * POS), 1)
    scale = HEAD ** -0.5
    lane = lax.broadcasted_iota(jnp.int32, (ROWS, 128), 1)
    loads[0].wait()
    loads[1].wait()

    def attend_pair(pair, start):
        request = group * REQ_DEV + pair * 2
        len_a, len_b = len_ref[request], len_ref[request + 1]
        used_a = lax.shift_right_logical(len_a + (POS - 1), 7)
        used_b = lax.shift_right_logical(len_b + (POS - 1), 7)
        slot = [jnp.minimum(start + i, SLOTS - 1) for i in range(PAIR_SLOTS)]
        keys = jnp.concatenate([k_ref[s] for s in slot], axis=1)
        values = jnp.concatenate([v_ref[s] for s in slot], axis=1)
        score = jnp.dot(q_ref[...], keys, preferred_element_type=jnp.float32) * scale
        edge = used_a * POS
        of_a = position < edge
        in_a = position < len_a
        in_b = jnp.logical_and(position >= edge, position < edge + len_b)
        max_a = jnp.max(jnp.where(in_a, score, FILL), axis=1, keepdims=True)
        max_b = jnp.max(jnp.where(in_b, score, FILL), axis=1, keepdims=True)
        term = jnp.exp(score - jnp.where(of_a, max_a, max_b))
        term_a = jnp.where(in_a, term, 0.0)
        term_b = jnp.where(in_b, term, 0.0)
        both = jnp.concatenate([term_a, term_b], axis=0)
        total = jnp.sum(both, axis=1, keepdims=True)
        acc = lax.dot_general(
            both.astype(jnp.bfloat16), values, (((1,), (1,)), ((), ())),
            preferred_element_type=jnp.float32,
        )
        row = pl.multiple_of(pair * (2 * TOKENS), 2 * TOKENS)
        att[pl.ds(row, 2 * TOKENS), 0:HEAD] = acc / total
        return start + used_a + used_b

    def attend():
        def step(i, start):
            for u in range(UNROLL):
                start = attend_pair(i * UNROLL + u, start)
            return start

        lax.fori_loop(0, PAIRS // UNROLL, step, 0)
        for q in range(TOKENS):
            first = att[pl.ds(q, ROWS, stride=TOKENS), :]
            second = att[pl.ds(ROWS * TOKENS + q, ROWS, stride=TOKENS), :]
            tile = jnp.where(lane < 64, first, pltpu.roll(second, 64, 1))
            tiles[q] = tile.astype(jnp.bfloat16)
        others[me] = tiles[me]

    def exchange():
        for offset in OFFSETS:
            to = peer(offset)
            pltpu.make_async_remote_copy(
                src_ref=tiles.at[to],
                dst_ref=others.at[me],
                send_sem=a2a_send,
                recv_sem=a2a_recv,
                device_id={"token": to},
                device_id_type=MESH,
            ).start()

    def all_tiles(ref, sem):
        some = ref.at[pl.ds(0, TOKENS - 1)]
        return pltpu.make_async_copy(some, some, sem)

    def mix(half):
        out = [None] * (WIDTH // 128)
        for j in range(TOKENS):
            x = tiles[j].astype(jnp.float32) + others[j].astype(jnp.float32)
            first = j * HEAD
            shift = first % 128
            turn = (shift + 64 * half) % 128
            if turn:
                x = pltpu.roll(x, turn, 1)
            t = first // 128
            if shift + HEAD > 128:
                out[t] = jnp.where(lane >= shift, x, out[t])
                out[t + 1] = x
            else:
                out[t] = x if out[t] is None else jnp.where(lane >= shift, x, out[t])
        normed = layer_norm(jnp.concatenate(out, axis=1)) * mix_gain[...].reshape(1, WIDTH)
        rows[half, y] = normed.astype(jnp.bfloat16)

    cols = (pl.ds(0, MID), pl.ds(MID, MID))
    sides = (slice(0, MID), slice(MID, WIDTH))

    def gather(half, way, kind, mine):
        sign = 1 - 2 * way
        reach = 1 + kind % 2
        source = (0, 0, -2, -2)[kind] if mine else (-1, -2, -3, -4)[kind]
        block = rows.at[half, at(sign * source)]
        if kind == 3:
            block = block.at[:, cols[way]]
        return pltpu.make_async_remote_copy(
            src_ref=block, dst_ref=block,
            send_sem=ag_send.at[half, way, kind], recv_sem=ag_recv.at[half, way, kind],
            device_id={"hidden": at(sign * reach)}, device_id_type=MESH,
        )

    def begin(half):
        for kind in (1, 0):
            for way in range(2):
                gather(half, way, kind, True).start()

    def forward(half):
        for way in range(2):
            gather(half, way, 1, False).wait_recv()
            for kind in (3, 2):
                gather(half, way, kind, True).start()

    def near(half):
        for way in range(2):
            gather(half, way, 0, False).wait_recv()

    def far(half):
        for kind in (2, 3):
            for way in range(2):
                gather(half, way, kind, False).wait_recv()

    ORDER = [0, -1, 1, -2, 2, -3, 3, 4]

    def ffn(half, first, last):
        x = jnp.concatenate(
            [rows[half, at(ORDER[i])] for i in range(first, last)], axis=0
        )
        up = jnp.dot(x, up_ref[...], preferred_element_type=jnp.float32)
        act = (0.5 * up * (1.0 + lax.erf(up * math.sqrt(0.5)))).astype(jnp.bfloat16)
        down = jnp.dot(act, down_ref[...], preferred_element_type=jnp.float32)
        part[half, first:last] = down.reshape(last - first, ROWS, WIDTH)

    def sums(half, way, kind):
        sign = 2 * way - 1
        src, dst = out_buf.at[half, way, kind], in_buf.at[half, way, kind]
        if kind == 2:
            src, dst = src.at[:, cols[way]], dst.at[:, cols[way]]
        return pltpu.make_async_remote_copy(
            src_ref=src, dst_ref=dst,
            send_sem=rs_send.at[half, way, kind], recv_sem=rs_recv.at[half, way, kind],
            device_id={"hidden": at(sign * (1, 1, 2, 2)[kind])}, device_id_type=MESH,
        )

    def scatter(half, kind):
        for way in range(2):
            if kind == 2:
                out_buf[half, way, 2, :, sides[way]] = part[half, 7, :, sides[way]].astype(jnp.bfloat16)
            elif kind == 3:
                sums(half, way, 2).wait_recv()
                sums(half, way, 1).wait_recv()
                for side in range(2):
                    c = sides[side]
                    x = part[half, 3 + way, :, c] + in_buf[half, way, 1, :, c].astype(jnp.float32)
                    if side == way:
                        x = x + in_buf[half, way, 2, :, c].astype(jnp.float32)
                    out_buf[half, way, 3, :, c] = x.astype(jnp.bfloat16)
            else:
                out_buf[half, way, kind] = part[half, (1, 5)[kind] + way].astype(jnp.bfloat16)
            sums(half, way, kind).start()

    def finish(half):
        total = part[half, 0] + rows[half, y].astype(jnp.float32)
        for kind in (0, 3):
            for way in range(2):
                sums(half, way, kind).wait_recv()
                total = total + in_buf[half, way, kind].astype(jnp.float32)
        out_ref[half * ROWS : (half + 1) * ROWS, :] = (
            layer_norm(total) * out_gain[...].reshape(1, WIDTH)
        ).astype(jnp.bfloat16)

    attend()
    pl.semaphore_wait(barrier, len(OFFSETS) + 4)
    exchange()
    all_tiles(others, a2a_recv).wait()
    for half in range(HALVES):
        mix(half)
        begin(half)
    loads[2].wait()
    loads[3].wait()
    forward(0)
    near(0)
    ffn(0, 0, 5)
    forward(1)
    scatter(0, 0)
    near(1)
    ffn(1, 0, 5)
    far(0)
    ffn(0, 5, 8)
    scatter(0, 2)
    scatter(0, 1)
    scatter(1, 0)
    far(1)
    ffn(1, 5, 8)
    scatter(1, 2)
    scatter(1, 1)
    scatter(0, 3)
    scatter(1, 3)
    finish(0)
    finish(1)

    all_tiles(tiles, a2a_send).wait()
    for half in range(HALVES):
        for way in range(2):
            for kind in range(4):
                gather(half, way, kind, True).wait_send()
                sums(half, way, kind).wait_send()


def local(hist_len, queries, history_keys, cached_history_values, gain_mix, w_up, w_down, gain_out):
    vmem = pl.BlockSpec(memory_space=pltpu.VMEM)
    hbm = pl.BlockSpec(memory_space=pl.ANY)
    bf16, f32 = jnp.bfloat16, jnp.float32
    dma = pltpu.SemaphoreType.DMA
    out = pl.pallas_call(
        kernel,
        out_shape=jax.ShapeDtypeStruct((REQ_DEV, WIDTH), bf16),
        in_specs=[pl.BlockSpec(memory_space=pltpu.SMEM), vmem, vmem, vmem, hbm, hbm, hbm, hbm],
        out_specs=vmem,
        scratch_shapes=[
            pltpu.VMEM((SLOTS, HEAD, POS), bf16),
            pltpu.VMEM((SLOTS, HEAD, POS), bf16),
            pltpu.VMEM(w_up.shape[1:], bf16),
            pltpu.VMEM(w_down.shape[1:], bf16),
            pltpu.VMEM((REQ_DEV * TOKENS, 128), f32),
            pltpu.VMEM((TOKENS, ROWS, 128), bf16),
            pltpu.VMEM((TOKENS, ROWS, 128), bf16),
            pltpu.VMEM((HALVES, RING, ROWS, WIDTH), bf16),
            pltpu.VMEM((HALVES, RING, ROWS, WIDTH), f32),
            pltpu.VMEM((HALVES, 2, 4, ROWS, WIDTH), bf16),
            pltpu.VMEM((HALVES, 2, 4, ROWS, WIDTH), bf16),
            dma((4,)),
            dma(()),
            dma(()),
            dma((HALVES, 2, 4)),
            dma((HALVES, 2, 4)),
            dma((HALVES, 2, 4)),
            dma((HALVES, 2, 4)),
        ],
        compiler_params=pltpu.CompilerParams(
            collective_id=0, has_side_effects=True, vmem_limit_bytes=60 * 2**20
        ),
        cost_estimate=pl.CostEstimate(
            flops=700_000_000, bytes_accessed=5_000_000, transcendentals=500_000
        ),
    )(
        hist_len, queries, gain_mix, gain_out,
        history_keys, cached_history_values, w_up, w_down,
    )
    return out.reshape(REQ_DEV, 1, WIDTH)


def solution(mesh):
    return jax.shard_map(
        local,
        mesh=mesh,
        in_specs=(
            P(),
            P(None, "token"),
            P(("batch", "hidden"), "token", None),
            P(("batch", "hidden"), "token", None),
            P(),
            P("token", None, "hidden"),
            P("token", "hidden", None),
            P(),
        ),
        out_specs=P(("batch", "hidden"), "token", None),
        check_vma=False,
    )
```

```python
import functools
import math

import jax
import jax.numpy as jnp
from jax import lax
from jax.experimental import pallas as pl
from jax.experimental.pallas import tpu as pltpu
from jax.sharding import PartitionSpec as P

TOKENS = 32
WIDTH = 1536
HEAD = 48
POS = 128
REQ_DEV = 32
SLOTS = 96
RING = 8
HALVES = 2
ROWS = REQ_DEV // HALVES
PAIR_SLOTS = 6
PAIRS = REQ_DEV // 2
GROUP = 16
MID = WIDTH // 2
KEEP = (0, 1, 1, 2, 3, 3)
FILL = -1e30
EPSILON = 1e-5
MESH = pl.DeviceIdType.MESH
SIDE = 8
OFFSETS = sorted(
    ((dx, dz) for dx in range(TOKENS // SIDE) for dz in range(SIDE) if dx or dz),
    key=lambda o: (-min(o[0], TOKENS // SIDE - o[0]) - min(o[1], SIDE - o[1]), o),
)


def layer_norm(x):
    mean = jnp.sum(x, axis=-1, keepdims=True) * (1.0 / WIDTH)
    c = x - mean
    var = jnp.sum(c * c, axis=-1, keepdims=True) * (1.0 / WIDTH)
    return c * lax.rsqrt(var + EPSILON)


def kernel(
    len_hbm, q_hbm, mix_hbm, gain_hbm, k_hbm, v_hbm, up_hbm, down_hbm,
    out_ref,
    len_ref, q_ref, mix_gain, out_gain, k_ref, v_ref, up_ref, down_ref, att, tiles, others, rows, part, out_buf, in_buf,
    load_sem, a2a_send, a2a_recv, ag_send, ag_recv, rs_send, rs_recv,
):
    me = lax.axis_index("token")
    y = lax.axis_index("hidden")
    group = lax.axis_index("batch") * RING + y

    def at(distance):
        return lax.rem(y + RING + distance, RING)


    def peer(offset):
        x, z = me // SIDE, lax.rem(me, SIDE)
        return lax.rem(x + offset[0], TOKENS // SIDE) * SIDE + lax.rem(z + offset[1], SIDE)

    barrier = pltpu.get_barrier_semaphore()
    for offset in OFFSETS:
        pl.semaphore_signal(
            barrier, inc=1, device_id={"token": peer(offset)}, device_id_type=MESH
        )
    for step in (2, -2, 1, -1):
        pl.semaphore_signal(
            barrier, inc=1, device_id={"hidden": at(step)}, device_id_type=MESH
        )

    loads = [
        pltpu.make_async_copy(k_hbm, k_ref, load_sem.at[0]),
        pltpu.make_async_copy(v_hbm, v_ref, load_sem.at[1]),
        pltpu.make_async_copy(up_hbm.at[0], up_ref, load_sem.at[2]),
        pltpu.make_async_copy(down_hbm.at[0], down_ref, load_sem.at[3]),
        pltpu.make_async_copy(len_hbm, len_ref, load_sem.at[4]),
        pltpu.make_async_copy(q_hbm, q_ref, load_sem.at[5]),
        pltpu.make_async_copy(mix_hbm, mix_gain, load_sem.at[6]),
        pltpu.make_async_copy(gain_hbm, out_gain, load_sem.at[7]),
    ]
    for i in (4, 5, 0, 1, 6, 7):
        loads[i].start()

    att[...] = jnp.zeros_like(att)
    position = lax.broadcasted_iota(jnp.int32, (1, PAIR_SLOTS * POS), 1)
    scale = HEAD ** -0.5
    lane = lax.broadcasted_iota(jnp.int32, (ROWS, 128), 1)
    for i in (4, 5, 0):
        loads[i].wait()
    loads[2].start()
    loads[3].start()

    def attend_group(first, start):
        lens, uses, slots, scores, terms, totals = [], [], [], [], [], []
        for i in range(GROUP):
            request = group * REQ_DEV + (first + i) * 2
            len_a, len_b = len_ref[request], len_ref[request + 1]
            used_a = lax.shift_right_logical(len_a + (POS - 1), 7)
            used_b = lax.shift_right_logical(len_b + (POS - 1), 7)
            lens.append((len_a, len_b))
            uses.append(used_a * POS)
            slots.append([jnp.minimum(start + i, SLOTS - 1) for i in range(PAIR_SLOTS)])
            start = start + used_a + used_b
        for i in range(GROUP):
            keys = jnp.concatenate([k_ref[s] for s in slots[i]], axis=1)
            scores.append(jnp.dot(q_ref[...], keys, preferred_element_type=jnp.float32) * scale)
        for i in range(GROUP):
            (len_a, len_b), edge = lens[i], uses[i]
            in_a = position < len_a
            in_b = jnp.logical_and(position >= edge, position < edge + len_b)
            max_a = jnp.max(jnp.where(in_a, scores[i], FILL), axis=1, keepdims=True)
            max_b = jnp.max(jnp.where(in_b, scores[i], FILL), axis=1, keepdims=True)
            term = jnp.exp(scores[i] - jnp.where(position < edge, max_a, max_b))
            both = jnp.concatenate(
                [jnp.where(in_a, term, 0.0), jnp.where(in_b, term, 0.0)], axis=0
            )
            totals.append(jnp.sum(both, axis=1, keepdims=True))
            terms.append(both.astype(jnp.bfloat16))
        if first == 0:
            loads[1].wait()
        for i in range(GROUP):
            values = jnp.concatenate([v_ref[s] for s in slots[i]], axis=1)
            acc = lax.dot_general(
                terms[i], values, (((1,), (1,)), ((), ())), preferred_element_type=jnp.float32
            )
            row = (first + i) * 2 * TOKENS
            att[row : row + 2 * TOKENS, 0:HEAD] = acc / totals[i]
        return start

    def attend():
        start = 0
        for first in range(0, PAIRS, GROUP):
            start = attend_group(first, start)
        for q in range(TOKENS):
            first = att[pl.ds(q, ROWS, stride=TOKENS), :]
            second = att[pl.ds(ROWS * TOKENS + q, ROWS, stride=TOKENS), :]
            tile = jnp.where(lane < 64, first, pltpu.roll(second, 64, 1))
            tiles[q] = tile.astype(jnp.bfloat16)
        others[me] = tiles[me]

    def exchange():
        for offset in OFFSETS:
            to = peer(offset)
            pltpu.make_async_remote_copy(
                src_ref=tiles.at[to],
                dst_ref=others.at[me],
                send_sem=a2a_send,
                recv_sem=a2a_recv,
                device_id={"token": to},
                device_id_type=MESH,
            ).start()

    def all_tiles(ref, sem):
        some = ref.at[pl.ds(0, TOKENS - 1)]
        return pltpu.make_async_copy(some, some, sem)

    def mix(half):
        out = [None] * (WIDTH // 128)
        for j in range(TOKENS):
            x = tiles[j].astype(jnp.float32) + others[j].astype(jnp.float32)
            first = j * HEAD
            shift = first % 128
            turn = (shift + 64 * half) % 128
            if turn:
                x = pltpu.roll(x, turn, 1)
            t = first // 128
            if shift + HEAD > 128:
                out[t] = jnp.where(lane >= shift, x, out[t])
                out[t + 1] = x
            else:
                out[t] = x if out[t] is None else jnp.where(lane >= shift, x, out[t])
        normed = layer_norm(jnp.concatenate(out, axis=1)) * mix_gain[...].reshape(1, WIDTH)
        rows[half, y] = normed.astype(jnp.bfloat16)

    cols = (pl.ds(0, MID), pl.ds(MID, MID))
    sides = (slice(0, MID), slice(MID, WIDTH))

    def gather(half, way, kind, mine):
        sign = 1 - 2 * way
        reach = (1, 2, 2, 1, 1, 2)[kind]
        source = (0, 0, 0, -2, -2, -2)[kind] - (0 if mine else reach)
        block = rows.at[half, at(sign * source)]
        if kind:
            block = block.at[:, cols[(0, 1, 0, 1, way)[kind - 1]]]
        return pltpu.make_async_remote_copy(
            src_ref=block, dst_ref=block,
            send_sem=ag_send.at[half, way, kind], recv_sem=ag_recv.at[half, way, kind],
            device_id={"hidden": at(sign * reach)}, device_id_type=MESH,
        )

    def begin(half):
        for turn in range(2):
            for way in range(2):
                gather(half, way, 1 + (way ^ turn), True).start()

    def begin_near(half):
        for way in range(2):
            gather(half, way, 0, True).start()

    def forward(half):
        for turn in range(2):
            for way in range(2):
                side = way ^ turn
                gather(half, way, 1 + side, False).wait_recv()
                if turn == 0:
                    gather(half, way, 5, True).start()
                gather(half, way, 3 + side, True).start()

    def near(half):
        for way in range(2):
            gather(half, way, 0, False).wait_recv()

    def far(half):
        for kind in (5, 3, 4):
            for way in range(2):
                gather(half, way, kind, False).wait_recv()

    ORDER = [0, -1, 1, -2, 2, -3, 3, 4]

    def ffn(half, first, last):
        x = jnp.concatenate(
            [rows[half, at(ORDER[i])] for i in range(first, last)], axis=0
        )
        up = jnp.dot(x, up_ref[...], preferred_element_type=jnp.float32)
        act = (0.5 * up * (1.0 + lax.erf(up * math.sqrt(0.5)))).astype(jnp.bfloat16)
        down = jnp.dot(act, down_ref[...], preferred_element_type=jnp.float32)
        part[half, first:last] = down.reshape(last - first, ROWS, WIDTH)

    def sums(half, way, kind):
        sign = 2 * way - 1
        src, dst = out_buf.at[half, way, KEEP[kind]], in_buf.at[half, way, KEEP[kind]]
        if kind:
            c = cols[(0, 1, way, 0, 1)[kind - 1]]
            src, dst = src.at[:, c], dst.at[:, c]
        return pltpu.make_async_remote_copy(
            src_ref=src, dst_ref=dst,
            send_sem=rs_send.at[half, way, kind], recv_sem=rs_recv.at[half, way, kind],
            device_id={"hidden": at(sign * (1, 1, 1, 2, 2, 2)[kind])}, device_id_type=MESH,
        )

    def put(half, way, kind, c, x):
        out_buf[half, way, KEEP[kind], :, c] = x.astype(jnp.bfloat16)
        sums(half, way, kind).start()

    def scatter_near(half):
        for way in range(2):
            put(half, way, 0, slice(0, WIDTH), part[half, 1 + way])

    def scatter(half):
        for way in range(2):
            c = sides[1 - way]
            put(half, way, 2 - way, c, part[half, 5 + way, :, c])
        for way in range(2):
            c = sides[way]
            put(half, way, 3, c, part[half, 7, :, c])
        for way in range(2):
            c = sides[way]
            put(half, way, 1 + way, c, part[half, 5 + way, :, c])

    def relay(half):
        for turn in range(2):
            for way in range(2):
                side = 1 - way if turn == 0 else way
                c = sides[side]
                sums(half, way, 1 + side).wait_recv()
                x = part[half, 3 + way, :, c] + in_buf[half, way, 1, :, c].astype(jnp.float32)
                if turn:
                    sums(half, way, 3).wait_recv()
                    x = x + in_buf[half, way, 2, :, c].astype(jnp.float32)
                put(half, way, 4 + side, c, x)

    def finish(half):
        total = part[half, 0] + rows[half, y].astype(jnp.float32)
        for way in range(2):
            sums(half, way, 0).wait_recv()
            total = total + in_buf[half, way, 0].astype(jnp.float32)
        for way in range(2):
            sums(half, way, 4).wait_recv()
            sums(half, way, 5).wait_recv()
            total = total + in_buf[half, way, 3].astype(jnp.float32)
        out_ref[half * ROWS : (half + 1) * ROWS, :] = (
            layer_norm(total) * out_gain[...].reshape(1, WIDTH)
        ).astype(jnp.bfloat16)

    attend()
    pl.semaphore_wait(barrier, len(OFFSETS) + 4)
    exchange()
    all_tiles(others, a2a_recv).wait()
    loads[6].wait()
    loads[7].wait()
    for half in range(HALVES):
        mix(half)
        begin(half)
    begin_near(0)
    begin_near(1)
    loads[2].wait()
    loads[3].wait()
    forward(0)
    forward(1)
    near(0)
    ffn(0, 0, 5)
    scatter_near(0)
    near(1)
    ffn(1, 0, 5)
    far(0)
    ffn(0, 5, 8)
    scatter(0)
    far(1)
    ffn(1, 5, 8)
    scatter(1)
    scatter_near(1)
    relay(0)
    relay(1)
    finish(0)
    finish(1)

    all_tiles(tiles, a2a_send).wait()
    for half in range(HALVES):
        for way in range(2):
            for kind in range(6):
                gather(half, way, kind, True).wait_send()
                sums(half, way, kind).wait_send()


def local(hist_len, queries, history_keys, cached_history_values, gain_mix, w_up, w_down, gain_out):
    vmem = pl.BlockSpec(memory_space=pltpu.VMEM)
    hbm = pl.BlockSpec(memory_space=pl.ANY)
    bf16, f32 = jnp.bfloat16, jnp.float32
    dma = pltpu.SemaphoreType.DMA
    out = pl.pallas_call(
        kernel,
        out_shape=pltpu.VMEM((REQ_DEV, WIDTH), bf16),
        in_specs=[hbm] * 8,
        out_specs=vmem,
        scratch_shapes=[
            pltpu.SMEM(hist_len.shape, hist_len.dtype),
            pltpu.VMEM(queries.shape, bf16),
            pltpu.VMEM(gain_mix.shape, f32),
            pltpu.VMEM(gain_out.shape, f32),
            pltpu.VMEM((SLOTS, HEAD, POS), bf16),
            pltpu.VMEM((SLOTS, HEAD, POS), bf16),
            pltpu.VMEM(w_up.shape[1:], bf16),
            pltpu.VMEM(w_down.shape[1:], bf16),
            pltpu.VMEM((REQ_DEV * TOKENS, 128), f32),
            pltpu.VMEM((TOKENS, ROWS, 128), bf16),
            pltpu.VMEM((TOKENS, ROWS, 128), bf16),
            pltpu.VMEM((HALVES, RING, ROWS, WIDTH), bf16),
            pltpu.VMEM((HALVES, RING, ROWS, WIDTH), f32),
            pltpu.VMEM((HALVES, 2, 4, ROWS, WIDTH), bf16),
            pltpu.VMEM((HALVES, 2, 4, ROWS, WIDTH), bf16),
            dma((8,)),
            dma(()),
            dma(()),
            dma((HALVES, 2, 6)),
            dma((HALVES, 2, 6)),
            dma((HALVES, 2, 6)),
            dma((HALVES, 2, 6)),
        ],
        compiler_params=pltpu.CompilerParams(
            collective_id=0, has_side_effects=True, vmem_limit_bytes=60 * 2**20
        ),
        cost_estimate=pl.CostEstimate(
            flops=700_000_000, bytes_accessed=5_000_000, transcendentals=500_000
        ),
    )(
        hist_len, queries, gain_mix, gain_out,
        history_keys, cached_history_values, w_up, w_down,
    )
    return out.reshape(REQ_DEV, 1, WIDTH)


def solution(mesh):
    return jax.shard_map(
        local,
        mesh=mesh,
        in_specs=(
            P(),
            P(None, "token"),
            P(("batch", "hidden"), "token", None),
            P(("batch", "hidden"), "token", None),
            P(),
            P("token", None, "hidden"),
            P("token", "hidden", None),
            P(),
        ),
        out_specs=P(("batch", "hidden"), "token", None),
        check_vma=False,
    )
```

```python
import functools
import math

import jax
import jax.numpy as jnp
from jax import lax
from jax.experimental import pallas as pl
from jax.experimental.pallas import tpu as pltpu
from jax.sharding import PartitionSpec as P

TOKENS = 32
WIDTH = 1536
HEAD = 48
POS = 128
REQ_DEV = 32
SLOTS = 96
RING = 8
HALVES = 2
ROWS = REQ_DEV // HALVES
PAIR_SLOTS = 6
PAIRS = REQ_DEV // 2
GROUP = 8
MID = WIDTH // 2
KEEP = (0, 1, 1, 2, 3, 3)
FILL = -1e30
EPSILON = 1e-5
MESH = pl.DeviceIdType.MESH
SIDE = 8
OFFSETS = sorted(
    ((dx, dz) for dx in range(TOKENS // SIDE) for dz in range(SIDE) if dx or dz),
    key=lambda o: (-min(o[0], TOKENS // SIDE - o[0]) - min(o[1], SIDE - o[1]), o),
)


def layer_norm(x):
    mean = jnp.sum(x, axis=-1, keepdims=True) * (1.0 / WIDTH)
    c = x - mean
    var = jnp.sum(c * c, axis=-1, keepdims=True) * (1.0 / WIDTH)
    return c * lax.rsqrt(var + EPSILON)


def kernel(
    len_hbm, q_hbm, mix_hbm, gain_hbm, k_hbm, v_hbm, up_hbm, down_hbm,
    out_ref,
    len_ref, q_ref, mix_gain, out_gain, k_ref, v_ref, up_ref, down_ref, att, tiles, others, rows, part, out_buf, in_buf,
    load_sem, a2a_send, a2a_recv, ag_send, ag_recv, rs_send, rs_recv,
):
    me = lax.axis_index("token")
    y = lax.axis_index("hidden")
    group = lax.axis_index("batch") * RING + y

    def at(distance):
        return lax.rem(y + RING + distance, RING)


    def peer(offset):
        x, z = me // SIDE, lax.rem(me, SIDE)
        return lax.rem(x + offset[0], TOKENS // SIDE) * SIDE + lax.rem(z + offset[1], SIDE)

    barrier = pltpu.get_barrier_semaphore()
    for offset in OFFSETS:
        pl.semaphore_signal(
            barrier, inc=1, device_id={"token": peer(offset)}, device_id_type=MESH
        )
    for step in (2, -2, 1, -1):
        pl.semaphore_signal(
            barrier, inc=1, device_id={"hidden": at(step)}, device_id_type=MESH
        )

    loads = [
        pltpu.make_async_copy(k_hbm, k_ref, load_sem.at[0]),
        pltpu.make_async_copy(v_hbm, v_ref, load_sem.at[1]),
        pltpu.make_async_copy(up_hbm.at[0], up_ref, load_sem.at[2]),
        pltpu.make_async_copy(down_hbm.at[0], down_ref, load_sem.at[3]),
        pltpu.make_async_copy(len_hbm, len_ref, load_sem.at[4]),
        pltpu.make_async_copy(q_hbm, q_ref, load_sem.at[5]),
        pltpu.make_async_copy(mix_hbm, mix_gain, load_sem.at[6]),
        pltpu.make_async_copy(gain_hbm, out_gain, load_sem.at[7]),
    ]
    for i in (4, 5, 0, 1, 6, 7):
        loads[i].start()

    att[...] = jnp.zeros_like(att)
    position = lax.broadcasted_iota(jnp.int32, (1, PAIR_SLOTS * POS), 1)
    scale = HEAD ** -0.5
    lane = lax.broadcasted_iota(jnp.int32, (ROWS, 128), 1)
    for i in (4, 5, 0):
        loads[i].wait()
    loads[2].start()
    loads[3].start()

    def attend_group(first, start):
        lens, uses, slots, scores, terms, totals = [], [], [], [], [], []
        for i in range(GROUP):
            request = group * REQ_DEV + (first + i) * 2
            len_a, len_b = len_ref[request], len_ref[request + 1]
            used_a = lax.shift_right_logical(len_a + (POS - 1), 7)
            used_b = lax.shift_right_logical(len_b + (POS - 1), 7)
            lens.append((len_a, len_b))
            uses.append(used_a * POS)
            slots.append([jnp.minimum(start + i, SLOTS - 1) for i in range(PAIR_SLOTS)])
            start = start + used_a + used_b
        for i in range(GROUP):
            keys = jnp.concatenate([k_ref[s] for s in slots[i]], axis=1)
            scores.append(jnp.dot(q_ref[...], keys, preferred_element_type=jnp.float32) * scale)
        for i in range(GROUP):
            (len_a, len_b), edge = lens[i], uses[i]
            in_a = position < len_a
            in_b = jnp.logical_and(position >= edge, position < edge + len_b)
            max_a = jnp.max(jnp.where(in_a, scores[i], FILL), axis=1, keepdims=True)
            max_b = jnp.max(jnp.where(in_b, scores[i], FILL), axis=1, keepdims=True)
            term = jnp.exp(scores[i] - jnp.where(position < edge, max_a, max_b))
            both = jnp.concatenate(
                [jnp.where(in_a, term, 0.0), jnp.where(in_b, term, 0.0)], axis=0
            )
            totals.append(jnp.sum(both, axis=1, keepdims=True))
            terms.append(both.astype(jnp.bfloat16))
        if first == 0:
            loads[1].wait()
        for i in range(GROUP):
            values = jnp.concatenate([v_ref[s] for s in slots[i]], axis=1)
            acc = lax.dot_general(
                terms[i], values, (((1,), (1,)), ((), ())), preferred_element_type=jnp.float32
            )
            row = (first + i) * 2 * TOKENS
            att[row : row + 2 * TOKENS, 0:HEAD] = acc / totals[i]
        return start

    def attend(half, start):
        for first in range(half * PAIRS // HALVES, (half + 1) * PAIRS // HALVES, GROUP):
            start = attend_group(first, start)
        for q in range(TOKENS):
            tile = att[pl.ds(half * ROWS * TOKENS + q, ROWS, stride=TOKENS), :]
            tiles[half, q] = tile.astype(jnp.bfloat16)
        others[half, me] = tiles[half, me]
        return start

    def exchange(half):
        for offset in OFFSETS:
            to = peer(offset)
            pltpu.make_async_remote_copy(
                src_ref=tiles.at[half, to],
                dst_ref=others.at[half, me],
                send_sem=a2a_send.at[half],
                recv_sem=a2a_recv.at[half],
                device_id={"token": to},
                device_id_type=MESH,
            ).start()

    def all_tiles(ref, half, sem):
        some = ref.at[half, pl.ds(0, TOKENS - 1)]
        return pltpu.make_async_copy(some, some, sem.at[half])

    def mix(half):
        out = [None] * (WIDTH // 128)
        for j in range(TOKENS):
            x = tiles[half, j].astype(jnp.float32) + others[half, j].astype(jnp.float32)
            first = j * HEAD
            shift = first % 128
            if shift:
                x = pltpu.roll(x, shift, 1)
            t = first // 128
            if shift + HEAD > 128:
                out[t] = jnp.where(lane >= shift, x, out[t])
                out[t + 1] = x
            else:
                out[t] = x if out[t] is None else jnp.where(lane >= shift, x, out[t])
        normed = layer_norm(jnp.concatenate(out, axis=1)) * mix_gain[...].reshape(1, WIDTH)
        rows[half, y] = normed.astype(jnp.bfloat16)

    cols = (pl.ds(0, MID), pl.ds(MID, MID))
    sides = (slice(0, MID), slice(MID, WIDTH))

    def gather(half, way, kind, mine):
        sign = 1 - 2 * way
        reach = (1, 2, 2, 1, 1, 2)[kind]
        source = (0, 0, 0, -2, -2, -2)[kind] - (0 if mine else reach)
        block = rows.at[half, at(sign * source)]
        if kind:
            block = block.at[:, cols[(0, 1, 0, 1, way)[kind - 1]]]
        return pltpu.make_async_remote_copy(
            src_ref=block, dst_ref=block,
            send_sem=ag_send.at[half, way, kind], recv_sem=ag_recv.at[half, way, kind],
            device_id={"hidden": at(sign * reach)}, device_id_type=MESH,
        )

    def begin(half):
        for turn in range(2):
            for way in range(2):
                gather(half, way, 1 + (way ^ turn), True).start()

    def begin_near(half):
        for way in range(2):
            gather(half, way, 0, True).start()

    def forward(half):
        for turn in range(2):
            for way in range(2):
                side = way ^ turn
                gather(half, way, 1 + side, False).wait_recv()
                if turn == 0:
                    gather(half, way, 5, True).start()
                gather(half, way, 3 + side, True).start()

    def near(half):
        for way in range(2):
            gather(half, way, 0, False).wait_recv()

    def far(half):
        for kind in (5, 3, 4):
            for way in range(2):
                gather(half, way, kind, False).wait_recv()

    ORDER = [0, -1, 1, -2, 2, -3, 3, 4]

    def ffn(half, first, last):
        x = jnp.concatenate(
            [rows[half, at(ORDER[i])] for i in range(first, last)], axis=0
        )
        up = jnp.dot(x, up_ref[...], preferred_element_type=jnp.float32)
        act = (0.5 * up * (1.0 + lax.erf(up * math.sqrt(0.5)))).astype(jnp.bfloat16)
        down = jnp.dot(act, down_ref[...], preferred_element_type=jnp.float32)
        part[half, first:last] = down.reshape(last - first, ROWS, WIDTH)

    def sums(half, way, kind):
        sign = 2 * way - 1
        src, dst = out_buf.at[half, way, KEEP[kind]], in_buf.at[half, way, KEEP[kind]]
        if kind:
            c = cols[(0, 1, way, 0, 1)[kind - 1]]
            src, dst = src.at[:, c], dst.at[:, c]
        return pltpu.make_async_remote_copy(
            src_ref=src, dst_ref=dst,
            send_sem=rs_send.at[half, way, kind], recv_sem=rs_recv.at[half, way, kind],
            device_id={"hidden": at(sign * (1, 1, 1, 2, 2, 2)[kind])}, device_id_type=MESH,
        )

    def put(half, way, kind, c, x):
        out_buf[half, way, KEEP[kind], :, c] = x.astype(jnp.bfloat16)
        sums(half, way, kind).start()

    def scatter_near(half):
        for way in range(2):
            put(half, way, 0, slice(0, WIDTH), part[half, 1 + way])

    def scatter(half):
        for way in range(2):
            c = sides[1 - way]
            put(half, way, 2 - way, c, part[half, 5 + way, :, c])
        for way in range(2):
            c = sides[way]
            put(half, way, 3, c, part[half, 7, :, c])
        for way in range(2):
            c = sides[way]
            put(half, way, 1 + way, c, part[half, 5 + way, :, c])

    def relay(half):
        for turn in range(2):
            for way in range(2):
                side = 1 - way if turn == 0 else way
                c = sides[side]
                sums(half, way, 1 + side).wait_recv()
                x = part[half, 3 + way, :, c] + in_buf[half, way, 1, :, c].astype(jnp.float32)
                if turn:
                    sums(half, way, 3).wait_recv()
                    x = x + in_buf[half, way, 2, :, c].astype(jnp.float32)
                put(half, way, 4 + side, c, x)

    def finish(half):
        total = part[half, 0] + rows[half, y].astype(jnp.float32)
        for way in range(2):
            sums(half, way, 0).wait_recv()
            total = total + in_buf[half, way, 0].astype(jnp.float32)
        for way in range(2):
            sums(half, way, 4).wait_recv()
            sums(half, way, 5).wait_recv()
            total = total + in_buf[half, way, 3].astype(jnp.float32)
        out_ref[half * ROWS : (half + 1) * ROWS, :] = (
            layer_norm(total) * out_gain[...].reshape(1, WIDTH)
        ).astype(jnp.bfloat16)

    start = attend(0, 0)
    pl.semaphore_wait(barrier, len(OFFSETS) + 4)
    exchange(0)
    attend(1, start)
    exchange(1)
    loads[6].wait()
    loads[7].wait()
    for half in range(HALVES):
        all_tiles(others, half, a2a_recv).wait()
        mix(half)
        begin(half)
        begin_near(half)
    loads[2].wait()
    loads[3].wait()
    forward(0)
    forward(1)
    near(0)
    ffn(0, 0, 5)
    scatter_near(0)
    near(1)
    ffn(1, 0, 5)
    far(0)
    ffn(0, 5, 8)
    scatter(0)
    far(1)
    ffn(1, 5, 8)
    scatter(1)
    scatter_near(1)
    relay(0)
    relay(1)
    finish(0)
    finish(1)

    for half in range(HALVES):
        all_tiles(tiles, half, a2a_send).wait()
        for way in range(2):
            for kind in range(6):
                gather(half, way, kind, True).wait_send()
                sums(half, way, kind).wait_send()


def local(hist_len, queries, history_keys, cached_history_values, gain_mix, w_up, w_down, gain_out):
    vmem = pl.BlockSpec(memory_space=pltpu.VMEM)
    hbm = pl.BlockSpec(memory_space=pl.ANY)
    bf16, f32 = jnp.bfloat16, jnp.float32
    dma = pltpu.SemaphoreType.DMA
    out = pl.pallas_call(
        kernel,
        out_shape=pltpu.VMEM((REQ_DEV, WIDTH), bf16),
        in_specs=[hbm] * 8,
        out_specs=vmem,
        scratch_shapes=[
            pltpu.SMEM(hist_len.shape, hist_len.dtype),
            pltpu.VMEM(queries.shape, bf16),
            pltpu.VMEM(gain_mix.shape, f32),
            pltpu.VMEM(gain_out.shape, f32),
            pltpu.VMEM((SLOTS, HEAD, POS), bf16),
            pltpu.VMEM((SLOTS, HEAD, POS), bf16),
            pltpu.VMEM(w_up.shape[1:], bf16),
            pltpu.VMEM(w_down.shape[1:], bf16),
            pltpu.VMEM((REQ_DEV * TOKENS, 128), f32),
            pltpu.VMEM((HALVES, TOKENS, ROWS, 128), bf16),
            pltpu.VMEM((HALVES, TOKENS, ROWS, 128), bf16),
            pltpu.VMEM((HALVES, RING, ROWS, WIDTH), bf16),
            pltpu.VMEM((HALVES, RING, ROWS, WIDTH), f32),
            pltpu.VMEM((HALVES, 2, 4, ROWS, WIDTH), bf16),
            pltpu.VMEM((HALVES, 2, 4, ROWS, WIDTH), bf16),
            dma((8,)),
            dma((HALVES,)),
            dma((HALVES,)),
            dma((HALVES, 2, 6)),
            dma((HALVES, 2, 6)),
            dma((HALVES, 2, 6)),
            dma((HALVES, 2, 6)),
        ],
        compiler_params=pltpu.CompilerParams(
            collective_id=0, has_side_effects=True, vmem_limit_bytes=60 * 2**20
        ),
        cost_estimate=pl.CostEstimate(
            flops=700_000_000, bytes_accessed=5_000_000, transcendentals=500_000
        ),
    )(
        hist_len, queries, gain_mix, gain_out,
        history_keys, cached_history_values, w_up, w_down,
    )
    return out.reshape(REQ_DEV, 1, WIDTH)


def solution(mesh):
    return jax.shard_map(
        local,
        mesh=mesh,
        in_specs=(
            P(),
            P(None, "token"),
            P(("batch", "hidden"), "token", None),
            P(("batch", "hidden"), "token", None),
            P(),
            P("token", None, "hidden"),
            P("token", "hidden", None),
            P(),
        ),
        out_specs=P(("batch", "hidden"), "token", None),
        check_vma=False,
    )
```

```python
import functools
import math

import jax
import jax.numpy as jnp
from jax import lax
from jax.experimental import pallas as pl
from jax.experimental.pallas import tpu as pltpu
from jax.sharding import PartitionSpec as P

TOKENS = 32
WIDTH = 1536
HEAD = 48
POS = 128
REQ_DEV = 32
SLOTS = 96
RING = 8
HALVES = 2
ROWS = REQ_DEV // HALVES
PAIR_SLOTS = 6
PAIRS = REQ_DEV // 2
GROUP = 8
MID = WIDTH // 2
KEEP = (0, 1, 1, 2, 3, 3)
FILL = -1e30
EPSILON = 1e-5
MESH = pl.DeviceIdType.MESH
SIDE = 8
OFFSETS = sorted(
    ((dx, dz) for dx in range(TOKENS // SIDE) for dz in range(SIDE) if dx or dz),
    key=lambda o: (-min(o[0], TOKENS // SIDE - o[0]) - min(o[1], SIDE - o[1]), o),
)


def layer_norm(x):
    mean = jnp.sum(x, axis=-1, keepdims=True) * (1.0 / WIDTH)
    c = x - mean
    var = jnp.sum(c * c, axis=-1, keepdims=True) * (1.0 / WIDTH)
    return c * lax.rsqrt(var + EPSILON)


def kernel(
    len_hbm, q_hbm, mix_hbm, gain_hbm, k_hbm, v_hbm, up_hbm, down_hbm,
    out_ref,
    len_ref, q_ref, mix_gain, out_gain, k_ref, v_ref, up_ref, down_ref, att, tiles, others, rows, part, out_buf, in_buf,
    load_sem, a2a_send, a2a_recv, ag_send, ag_recv, rs_send, rs_recv,
):
    me = lax.axis_index("token")
    y = lax.axis_index("hidden")
    group = lax.axis_index("batch") * RING + y

    def at(distance):
        return lax.rem(y + RING + distance, RING)


    def peer(offset):
        x, z = me // SIDE, lax.rem(me, SIDE)
        return lax.rem(x + offset[0], TOKENS // SIDE) * SIDE + lax.rem(z + offset[1], SIDE)

    barrier = pltpu.get_barrier_semaphore()
    for offset in OFFSETS:
        pl.semaphore_signal(
            barrier, inc=1, device_id={"token": peer(offset)}, device_id_type=MESH
        )
    for step in (2, -2, 1, -1):
        pl.semaphore_signal(
            barrier, inc=1, device_id={"hidden": at(step)}, device_id_type=MESH
        )

    loads = [
        pltpu.make_async_copy(k_hbm, k_ref, load_sem.at[0]),
        pltpu.make_async_copy(v_hbm, v_ref, load_sem.at[1]),
        pltpu.make_async_copy(up_hbm.at[0], up_ref, load_sem.at[2]),
        pltpu.make_async_copy(down_hbm.at[0], down_ref, load_sem.at[3]),
        pltpu.make_async_copy(len_hbm, len_ref, load_sem.at[4]),
        pltpu.make_async_copy(q_hbm, q_ref, load_sem.at[5]),
        pltpu.make_async_copy(mix_hbm, mix_gain, load_sem.at[6]),
        pltpu.make_async_copy(gain_hbm, out_gain, load_sem.at[7]),
    ]
    for i in (4, 5, 0, 1, 6, 7):
        loads[i].start()

    att[...] = jnp.zeros_like(att)
    position = lax.broadcasted_iota(jnp.int32, (1, PAIR_SLOTS * POS), 1)
    scale = HEAD ** -0.5
    lane = lax.broadcasted_iota(jnp.int32, (ROWS, 128), 1)
    for i in (4, 5, 0):
        loads[i].wait()
    loads[2].start()
    loads[3].start()

    def attend_group(first, start):
        lens, uses, slots, scores, terms, totals = [], [], [], [], [], []
        for i in range(GROUP):
            request = group * REQ_DEV + (first + i) * 2
            len_a, len_b = len_ref[request], len_ref[request + 1]
            used_a = lax.shift_right_logical(len_a + (POS - 1), 7)
            used_b = lax.shift_right_logical(len_b + (POS - 1), 7)
            lens.append((len_a, len_b))
            uses.append(used_a * POS)
            slots.append([jnp.minimum(start + i, SLOTS - 1) for i in range(PAIR_SLOTS)])
            start = start + used_a + used_b
        for i in range(GROUP):
            keys = jnp.concatenate([k_ref[s] for s in slots[i]], axis=1)
            scores.append(jnp.dot(q_ref[...], keys, preferred_element_type=jnp.float32) * scale)
        for i in range(GROUP):
            (len_a, len_b), edge = lens[i], uses[i]
            in_a = position < len_a
            in_b = jnp.logical_and(position >= edge, position < edge + len_b)
            max_a = jnp.max(jnp.where(in_a, scores[i], FILL), axis=1, keepdims=True)
            max_b = jnp.max(jnp.where(in_b, scores[i], FILL), axis=1, keepdims=True)
            term = jnp.exp(scores[i] - jnp.where(position < edge, max_a, max_b))
            both = jnp.concatenate(
                [jnp.where(in_a, term, 0.0), jnp.where(in_b, term, 0.0)], axis=0
            )
            totals.append(jnp.sum(both, axis=1, keepdims=True))
            terms.append(both.astype(jnp.bfloat16))
        if first == 0:
            loads[1].wait()
        for i in range(GROUP):
            values = jnp.concatenate([v_ref[s] for s in slots[i]], axis=1)
            acc = lax.dot_general(
                terms[i], values, (((1,), (1,)), ((), ())), preferred_element_type=jnp.float32
            )
            row = (first + i) * 2 * TOKENS
            att[row : row + 2 * TOKENS, 0:HEAD] = acc / totals[i]
        return start

    def attend(half, start):
        for first in range(half * PAIRS // HALVES, (half + 1) * PAIRS // HALVES, GROUP):
            start = attend_group(first, start)
        for q in range(TOKENS):
            tile = att[pl.ds(half * ROWS * TOKENS + q, ROWS, stride=TOKENS), :]
            tiles[half, q] = tile.astype(jnp.bfloat16)
        others[half, me] = tiles[half, me]
        return start

    def exchange(half):
        for offset in OFFSETS:
            to = peer(offset)
            pltpu.make_async_remote_copy(
                src_ref=tiles.at[half, to],
                dst_ref=others.at[half, me],
                send_sem=a2a_send.at[half],
                recv_sem=a2a_recv.at[half],
                device_id={"token": to},
                device_id_type=MESH,
            ).start()

    def all_tiles(ref, half, sem):
        some = ref.at[half, pl.ds(0, TOKENS - 1)]
        return pltpu.make_async_copy(some, some, sem.at[half])

    def mix(half):
        out = [None] * (WIDTH // 128)
        for j in range(TOKENS):
            x = tiles[half, j].astype(jnp.float32) + others[half, j].astype(jnp.float32)
            first = j * HEAD
            shift = first % 128
            if shift:
                x = pltpu.roll(x, shift, 1)
            t = first // 128
            if shift + HEAD > 128:
                out[t] = jnp.where(lane >= shift, x, out[t])
                out[t + 1] = x
            else:
                out[t] = x if out[t] is None else jnp.where(lane >= shift, x, out[t])
        normed = layer_norm(jnp.concatenate(out, axis=1)) * mix_gain[...].reshape(1, WIDTH)
        rows[half, y] = normed.astype(jnp.bfloat16)

    cols = (pl.ds(0, MID), pl.ds(MID, MID))
    sides = (slice(0, MID), slice(MID, WIDTH))

    def gather(half, way, kind, mine):
        sign = 1 - 2 * way
        reach = (1, 2, 2, 1, 1, 2)[kind]
        source = (0, 0, 0, -2, -2, -2)[kind] - (0 if mine else reach)
        block = rows.at[half, at(sign * source)]
        if kind:
            block = block.at[:, cols[(0, 1, 0, 1, way)[kind - 1]]]
        return pltpu.make_async_remote_copy(
            src_ref=block, dst_ref=block,
            send_sem=ag_send.at[half, way, kind], recv_sem=ag_recv.at[half, way, kind],
            device_id={"hidden": at(sign * reach)}, device_id_type=MESH,
        )

    def begin(half):
        for turn in range(2):
            for way in range(2):
                gather(half, way, 1 + (way ^ turn), True).start()

    def begin_near(half):
        for way in range(2):
            gather(half, way, 0, True).start()

    def forward(half):
        for turn in range(2):
            for way in range(2):
                side = way ^ turn
                gather(half, way, 1 + side, False).wait_recv()
                if turn == 0:
                    gather(half, way, 5, True).start()
                gather(half, way, 3 + side, True).start()

    def near(half):
        for way in range(2):
            gather(half, way, 0, False).wait_recv()

    def far(half):
        for kind in (5, 3, 4):
            for way in range(2):
                gather(half, way, kind, False).wait_recv()

    ORDER = [0, -1, 1, -2, 2, -3, 3, 4]

    def ffn(half, first, last):
        x = jnp.concatenate(
            [rows[half, at(ORDER[i])] for i in range(first, last)], axis=0
        )
        up = jnp.dot(x, up_ref[...], preferred_element_type=jnp.float32)
        act = (0.5 * up * (1.0 + lax.erf(up * math.sqrt(0.5)))).astype(jnp.bfloat16)
        down = jnp.dot(act, down_ref[...], preferred_element_type=jnp.float32)
        part[half, first:last] = down.reshape(last - first, ROWS, WIDTH)

    def sums(half, way, kind):
        sign = 2 * way - 1
        src, dst = out_buf.at[half, way, KEEP[kind]], in_buf.at[half, way, KEEP[kind]]
        if kind:
            c = cols[(0, 1, way, 0, 1)[kind - 1]]
            src, dst = src.at[:, c], dst.at[:, c]
        return pltpu.make_async_remote_copy(
            src_ref=src, dst_ref=dst,
            send_sem=rs_send.at[half, way, kind], recv_sem=rs_recv.at[half, way, kind],
            device_id={"hidden": at(sign * (1, 1, 1, 2, 2, 2)[kind])}, device_id_type=MESH,
        )

    def put(half, way, kind, c, x):
        out_buf[half, way, KEEP[kind], :, c] = x.astype(jnp.bfloat16)
        sums(half, way, kind).start()

    def scatter_near(half):
        for way in range(2):
            put(half, way, 0, slice(0, WIDTH), part[half, 1 + way])

    def scatter(half):
        for way in range(2):
            c = sides[1 - way]
            put(half, way, 2 - way, c, part[half, 5 + way, :, c])
        for way in range(2):
            c = sides[way]
            put(half, way, 3, c, part[half, 7, :, c])
        for way in range(2):
            c = sides[way]
            put(half, way, 1 + way, c, part[half, 5 + way, :, c])

    def relay(half):
        for turn in range(2):
            for way in range(2):
                side = 1 - way if turn == 0 else way
                c = sides[side]
                sums(half, way, 1 + side).wait_recv()
                x = part[half, 3 + way, :, c] + in_buf[half, way, 1, :, c].astype(jnp.float32)
                if turn:
                    sums(half, way, 3).wait_recv()
                    x = x + in_buf[half, way, 2, :, c].astype(jnp.float32)
                put(half, way, 4 + side, c, x)

    def finish(half):
        total = part[half, 0] + rows[half, y].astype(jnp.float32)
        for way in range(2):
            sums(half, way, 0).wait_recv()
            total = total + in_buf[half, way, 0].astype(jnp.float32)
        for way in range(2):
            sums(half, way, 4).wait_recv()
            sums(half, way, 5).wait_recv()
            total = total + in_buf[half, way, 3].astype(jnp.float32)
        out_ref[half * ROWS : (half + 1) * ROWS, :] = (
            layer_norm(total) * out_gain[...].reshape(1, WIDTH)
        ).astype(jnp.bfloat16)

    start = attend(0, 0)
    pl.semaphore_wait(barrier, len(OFFSETS) + 4)
    exchange(0)
    attend(1, start)
    exchange(1)
    loads[6].wait()
    loads[7].wait()
    for half in range(HALVES):
        all_tiles(others, half, a2a_recv).wait()
        mix(half)
        begin(half)
        begin_near(half)
    loads[2].wait()
    loads[3].wait()
    forward(0)
    near(0)
    ffn(0, 0, 5)
    forward(1)
    scatter_near(0)
    near(1)
    ffn(1, 0, 5)
    far(0)
    ffn(0, 5, 8)
    scatter(0)
    far(1)
    ffn(1, 5, 8)
    scatter(1)
    scatter_near(1)
    relay(0)
    relay(1)
    finish(0)
    finish(1)

    for half in range(HALVES):
        all_tiles(tiles, half, a2a_send).wait()
        for way in range(2):
            for kind in range(6):
                gather(half, way, kind, True).wait_send()
                sums(half, way, kind).wait_send()


def local(hist_len, queries, history_keys, cached_history_values, gain_mix, w_up, w_down, gain_out):
    vmem = pl.BlockSpec(memory_space=pltpu.VMEM)
    hbm = pl.BlockSpec(memory_space=pl.ANY)
    bf16, f32 = jnp.bfloat16, jnp.float32
    dma = pltpu.SemaphoreType.DMA
    out = pl.pallas_call(
        kernel,
        out_shape=pltpu.VMEM((REQ_DEV, WIDTH), bf16),
        in_specs=[hbm] * 8,
        out_specs=vmem,
        scratch_shapes=[
            pltpu.SMEM(hist_len.shape, hist_len.dtype),
            pltpu.VMEM(queries.shape, bf16),
            pltpu.VMEM(gain_mix.shape, f32),
            pltpu.VMEM(gain_out.shape, f32),
            pltpu.VMEM((SLOTS, HEAD, POS), bf16),
            pltpu.VMEM((SLOTS, HEAD, POS), bf16),
            pltpu.VMEM(w_up.shape[1:], bf16),
            pltpu.VMEM(w_down.shape[1:], bf16),
            pltpu.VMEM((REQ_DEV * TOKENS, 128), f32),
            pltpu.VMEM((HALVES, TOKENS, ROWS, 128), bf16),
            pltpu.VMEM((HALVES, TOKENS, ROWS, 128), bf16),
            pltpu.VMEM((HALVES, RING, ROWS, WIDTH), bf16),
            pltpu.VMEM((HALVES, RING, ROWS, WIDTH), f32),
            pltpu.VMEM((HALVES, 2, 4, ROWS, WIDTH), bf16),
            pltpu.VMEM((HALVES, 2, 4, ROWS, WIDTH), bf16),
            dma((8,)),
            dma((HALVES,)),
            dma((HALVES,)),
            dma((HALVES, 2, 6)),
            dma((HALVES, 2, 6)),
            dma((HALVES, 2, 6)),
            dma((HALVES, 2, 6)),
        ],
        compiler_params=pltpu.CompilerParams(
            collective_id=0, has_side_effects=True, vmem_limit_bytes=60 * 2**20
        ),
        cost_estimate=pl.CostEstimate(
            flops=700_000_000, bytes_accessed=5_000_000, transcendentals=500_000
        ),
    )(
        hist_len, queries, gain_mix, gain_out,
        history_keys, cached_history_values, w_up, w_down,
    )
    return out.reshape(REQ_DEV, 1, WIDTH)


def solution(mesh):
    return jax.shard_map(
        local,
        mesh=mesh,
        in_specs=(
            P(),
            P(None, "token"),
            P(("batch", "hidden"), "token", None),
            P(("batch", "hidden"), "token", None),
            P(),
            P("token", None, "hidden"),
            P("token", "hidden", None),
            P(),
        ),
        out_specs=P(("batch", "hidden"), "token", None),
        check_vma=False,
    )
```

```python
import functools
import math

import jax
import jax.numpy as jnp
from jax import lax
from jax.experimental import pallas as pl
from jax.experimental.pallas import tpu as pltpu
from jax.sharding import PartitionSpec as P

TOKENS = 32
WIDTH = 1536
HEAD = 48
POS = 128
REQ_DEV = 32
SLOTS = 96
RING = 8
HALVES = 2
ROWS = REQ_DEV // HALVES
PAIR_SLOTS = 6
PAIRS = REQ_DEV // 2
GROUP = 8
MID = WIDTH // 2
KEEP = (0, 1, 1, 2, 3, 3)
FILL = -1e30
EPSILON = 1e-5
MESH = pl.DeviceIdType.MESH
SIDE = 8
OFFSETS = sorted(
    ((dx, dz) for dx in range(TOKENS // SIDE) for dz in range(SIDE) if dx or dz),
    key=lambda o: (-min(o[0], TOKENS // SIDE - o[0]) - min(o[1], SIDE - o[1]), o),
)


def layer_norm(x):
    mean = jnp.sum(x, axis=-1, keepdims=True) * (1.0 / WIDTH)
    c = x - mean
    var = jnp.sum(c * c, axis=-1, keepdims=True) * (1.0 / WIDTH)
    return c * lax.rsqrt(var + EPSILON)


def kernel(
    len_hbm, q_hbm, mix_hbm, gain_hbm, k_hbm, v_hbm, up_hbm, down_hbm,
    out_ref,
    len_ref, q_ref, mix_gain, out_gain, k_ref, v_ref, up_ref, down_ref, att, tiles, others, rows, part, out_buf, in_buf,
    load_sem, a2a_send, a2a_recv, ag_send, ag_recv, rs_send, rs_recv,
):
    me = lax.axis_index("token")
    y = lax.axis_index("hidden")
    group = lax.axis_index("batch") * RING + y

    def at(distance):
        return lax.rem(y + RING + distance, RING)


    def peer(offset):
        x, z = me // SIDE, lax.rem(me, SIDE)
        return lax.rem(x + offset[0], TOKENS // SIDE) * SIDE + lax.rem(z + offset[1], SIDE)

    barrier = pltpu.get_barrier_semaphore()
    for offset in OFFSETS:
        pl.semaphore_signal(
            barrier, inc=1, device_id={"token": peer(offset)}, device_id_type=MESH
        )
    for step in (2, -2, 1, -1):
        pl.semaphore_signal(
            barrier, inc=1, device_id={"hidden": at(step)}, device_id_type=MESH
        )

    loads = [
        pltpu.make_async_copy(k_hbm, k_ref, load_sem.at[0]),
        pltpu.make_async_copy(v_hbm, v_ref, load_sem.at[1]),
        pltpu.make_async_copy(up_hbm.at[0], up_ref, load_sem.at[2]),
        pltpu.make_async_copy(down_hbm.at[0], down_ref, load_sem.at[3]),
        pltpu.make_async_copy(len_hbm, len_ref, load_sem.at[4]),
        pltpu.make_async_copy(q_hbm, q_ref, load_sem.at[5]),
        pltpu.make_async_copy(mix_hbm, mix_gain, load_sem.at[6]),
        pltpu.make_async_copy(gain_hbm, out_gain, load_sem.at[7]),
    ]
    for i in (4, 5, 0, 1, 6, 7):
        loads[i].start()

    att[...] = jnp.zeros_like(att)
    position = lax.broadcasted_iota(jnp.int32, (1, PAIR_SLOTS * POS), 1)
    scale = HEAD ** -0.5
    lane = lax.broadcasted_iota(jnp.int32, (ROWS, 128), 1)
    for i in (4, 5, 0):
        loads[i].wait()
    loads[2].start()
    loads[3].start()

    def attend_group(first, start):
        lens, uses, slots, scores, terms, totals = [], [], [], [], [], []
        for i in range(GROUP):
            request = group * REQ_DEV + (first + i) * 2
            len_a, len_b = len_ref[request], len_ref[request + 1]
            used_a = lax.shift_right_logical(len_a + (POS - 1), 7)
            used_b = lax.shift_right_logical(len_b + (POS - 1), 7)
            lens.append((len_a, len_b))
            uses.append(used_a * POS)
            slots.append([jnp.minimum(start + i, SLOTS - 1) for i in range(PAIR_SLOTS)])
            start = start + used_a + used_b
        for i in range(GROUP):
            keys = jnp.concatenate([k_ref[s] for s in slots[i]], axis=1)
            scores.append(jnp.dot(q_ref[...], keys, preferred_element_type=jnp.float32) * scale)
        for i in range(GROUP):
            (len_a, len_b), edge = lens[i], uses[i]
            in_a = position < len_a
            in_b = jnp.logical_and(position >= edge, position < edge + len_b)
            max_a = jnp.max(jnp.where(in_a, scores[i], FILL), axis=1, keepdims=True)
            max_b = jnp.max(jnp.where(in_b, scores[i], FILL), axis=1, keepdims=True)
            term = jnp.exp(scores[i] - jnp.where(position < edge, max_a, max_b))
            both = jnp.concatenate(
                [jnp.where(in_a, term, 0.0), jnp.where(in_b, term, 0.0)], axis=0
            )
            totals.append(jnp.sum(both, axis=1, keepdims=True))
            terms.append(both.astype(jnp.bfloat16))
        if first == 0:
            loads[1].wait()
        for i in range(GROUP):
            values = jnp.concatenate([v_ref[s] for s in slots[i]], axis=1)
            acc = lax.dot_general(
                terms[i], values, (((1,), (1,)), ((), ())), preferred_element_type=jnp.float32
            )
            row = (first + i) * 2 * TOKENS
            att[row : row + 2 * TOKENS, 0:HEAD] = acc / totals[i]
        return start

    def attend(half, start):
        for first in range(half * PAIRS // HALVES, (half + 1) * PAIRS // HALVES, GROUP):
            start = attend_group(first, start)
        for q in range(TOKENS):
            tile = att[pl.ds(half * ROWS * TOKENS + q, ROWS, stride=TOKENS), :]
            tiles[half, q] = tile.astype(jnp.bfloat16)
        others[half, me] = tiles[half, me]
        return start

    def exchange(half):
        for offset in OFFSETS:
            to = peer(offset)
            pltpu.make_async_remote_copy(
                src_ref=tiles.at[half, to],
                dst_ref=others.at[half, me],
                send_sem=a2a_send.at[half],
                recv_sem=a2a_recv.at[half],
                device_id={"token": to},
                device_id_type=MESH,
            ).start()

    def all_tiles(ref, half, sem):
        some = ref.at[half, pl.ds(0, TOKENS - 1)]
        return pltpu.make_async_copy(some, some, sem.at[half])

    def mix(half):
        out = [None] * (WIDTH // 128)
        for j in range(TOKENS):
            x = tiles[half, j].astype(jnp.float32) + others[half, j].astype(jnp.float32)
            first = j * HEAD
            shift = first % 128
            if shift:
                x = pltpu.roll(x, shift, 1)
            t = first // 128
            if shift + HEAD > 128:
                out[t] = jnp.where(lane >= shift, x, out[t])
                out[t + 1] = x
            else:
                out[t] = x if out[t] is None else jnp.where(lane >= shift, x, out[t])
        normed = layer_norm(jnp.concatenate(out, axis=1)) * mix_gain[...].reshape(1, WIDTH)
        rows[half, y] = normed.astype(jnp.bfloat16)

    cols = (pl.ds(0, MID), pl.ds(MID, MID))
    sides = (slice(0, MID), slice(MID, WIDTH))

    def gather(half, way, kind, mine):
        sign = 1 - 2 * way
        reach = (1, 2, 2, 1, 1, 2)[kind]
        source = (0, 0, 0, -2, -2, -2)[kind] - (0 if mine else reach)
        block = rows.at[half, at(sign * source)]
        if kind:
            block = block.at[:, cols[(0, 1, 0, 1, way)[kind - 1]]]
        return pltpu.make_async_remote_copy(
            src_ref=block, dst_ref=block,
            send_sem=ag_send.at[half, way, kind], recv_sem=ag_recv.at[half, way, kind],
            device_id={"hidden": at(sign * reach)}, device_id_type=MESH,
        )

    def begin(half):
        for turn in range(2):
            for way in range(2):
                gather(half, way, 1 + (way ^ turn), True).start()

    def begin_near(half):
        for way in range(2):
            gather(half, way, 0, True).start()

    def forward(half):
        for turn in range(2):
            for way in range(2):
                side = way ^ turn
                gather(half, way, 1 + side, False).wait_recv()
                if turn == 0:
                    gather(half, way, 5, True).start()
                gather(half, way, 3 + side, True).start()

    def near(half):
        for way in range(2):
            gather(half, way, 0, False).wait_recv()

    def far(half):
        for kind in (5, 3, 4):
            for way in range(2):
                gather(half, way, kind, False).wait_recv()

    ORDER = [0, -1, 1, -2, 2, -3, 3, 4]

    def ffn(half, first, last):
        x = jnp.concatenate(
            [rows[half, at(ORDER[i])] for i in range(first, last)], axis=0
        )
        up = jnp.dot(x, up_ref[...], preferred_element_type=jnp.float32)
        act = (0.5 * up * (1.0 + lax.erf(up * math.sqrt(0.5)))).astype(jnp.bfloat16)
        down = jnp.dot(act, down_ref[...], preferred_element_type=jnp.float32)
        part[half, first:last] = down.reshape(last - first, ROWS, WIDTH)

    def sums(half, way, kind):
        sign = 2 * way - 1
        src, dst = out_buf.at[half, way, KEEP[kind]], in_buf.at[half, way, KEEP[kind]]
        if kind:
            c = cols[(0, 1, way, 0, 1)[kind - 1]]
            src, dst = src.at[:, c], dst.at[:, c]
        return pltpu.make_async_remote_copy(
            src_ref=src, dst_ref=dst,
            send_sem=rs_send.at[half, way, kind], recv_sem=rs_recv.at[half, way, kind],
            device_id={"hidden": at(sign * (1, 1, 1, 2, 2, 2)[kind])}, device_id_type=MESH,
        )

    def put(half, way, kind, c, x):
        out_buf[half, way, KEEP[kind], :, c] = x.astype(jnp.bfloat16)
        sums(half, way, kind).start()

    def scatter_near(half):
        for way in range(2):
            put(half, way, 0, slice(0, WIDTH), part[half, 1 + way])

    def scatter(half):
        for way in range(2):
            c = sides[1 - way]
            put(half, way, 2 - way, c, part[half, 5 + way, :, c])
        for way in range(2):
            c = sides[way]
            put(half, way, 3, c, part[half, 7, :, c])
        for way in range(2):
            c = sides[way]
            put(half, way, 1 + way, c, part[half, 5 + way, :, c])

    def relay(half):
        for turn in range(2):
            for way in range(2):
                side = 1 - way if turn == 0 else way
                c = sides[side]
                sums(half, way, 1 + side).wait_recv()
                x = part[half, 3 + way, :, c] + in_buf[half, way, 1, :, c].astype(jnp.float32)
                if turn:
                    sums(half, way, 3).wait_recv()
                    x = x + in_buf[half, way, 2, :, c].astype(jnp.float32)
                put(half, way, 4 + side, c, x)

    def finish(half):
        total = part[half, 0] + rows[half, y].astype(jnp.float32)
        for way in range(2):
            sums(half, way, 0).wait_recv()
            total = total + in_buf[half, way, 0].astype(jnp.float32)
        for way in range(2):
            sums(half, way, 4).wait_recv()
            sums(half, way, 5).wait_recv()
            total = total + in_buf[half, way, 3].astype(jnp.float32)
        out_ref[half * ROWS : (half + 1) * ROWS, :] = (
            layer_norm(total) * out_gain[...].reshape(1, WIDTH)
        ).astype(jnp.bfloat16)

    start = attend(0, 0)
    pl.semaphore_wait(barrier, len(OFFSETS) + 4)
    exchange(0)
    attend(1, start)
    exchange(1)
    loads[6].wait()
    loads[7].wait()
    for half in range(HALVES):
        all_tiles(others, half, a2a_recv).wait()
        mix(half)
        begin(half)
        begin_near(half)
    loads[2].wait()
    loads[3].wait()
    forward(0)
    forward(1)
    near(0)
    ffn(0, 0, 5)
    scatter_near(0)
    far(0)
    ffn(0, 5, 8)
    scatter(0)
    far(1)
    ffn(1, 5, 8)
    scatter(1)
    near(1)
    ffn(1, 0, 5)
    scatter_near(1)
    relay(0)
    relay(1)
    finish(0)
    finish(1)

    for half in range(HALVES):
        all_tiles(tiles, half, a2a_send).wait()
        for way in range(2):
            for kind in range(6):
                gather(half, way, kind, True).wait_send()
                sums(half, way, kind).wait_send()


def local(hist_len, queries, history_keys, cached_history_values, gain_mix, w_up, w_down, gain_out):
    vmem = pl.BlockSpec(memory_space=pltpu.VMEM)
    hbm = pl.BlockSpec(memory_space=pl.ANY)
    bf16, f32 = jnp.bfloat16, jnp.float32
    dma = pltpu.SemaphoreType.DMA
    out = pl.pallas_call(
        kernel,
        out_shape=pltpu.VMEM((REQ_DEV, WIDTH), bf16),
        in_specs=[hbm] * 8,
        out_specs=vmem,
        scratch_shapes=[
            pltpu.SMEM(hist_len.shape, hist_len.dtype),
            pltpu.VMEM(queries.shape, bf16),
            pltpu.VMEM(gain_mix.shape, f32),
            pltpu.VMEM(gain_out.shape, f32),
            pltpu.VMEM((SLOTS, HEAD, POS), bf16),
            pltpu.VMEM((SLOTS, HEAD, POS), bf16),
            pltpu.VMEM(w_up.shape[1:], bf16),
            pltpu.VMEM(w_down.shape[1:], bf16),
            pltpu.VMEM((REQ_DEV * TOKENS, 128), f32),
            pltpu.VMEM((HALVES, TOKENS, ROWS, 128), bf16),
            pltpu.VMEM((HALVES, TOKENS, ROWS, 128), bf16),
            pltpu.VMEM((HALVES, RING, ROWS, WIDTH), bf16),
            pltpu.VMEM((HALVES, RING, ROWS, WIDTH), f32),
            pltpu.VMEM((HALVES, 2, 4, ROWS, WIDTH), bf16),
            pltpu.VMEM((HALVES, 2, 4, ROWS, WIDTH), bf16),
            dma((8,)),
            dma((HALVES,)),
            dma((HALVES,)),
            dma((HALVES, 2, 6)),
            dma((HALVES, 2, 6)),
            dma((HALVES, 2, 6)),
            dma((HALVES, 2, 6)),
        ],
        compiler_params=pltpu.CompilerParams(
            collective_id=0, has_side_effects=True, vmem_limit_bytes=60 * 2**20
        ),
        cost_estimate=pl.CostEstimate(
            flops=700_000_000, bytes_accessed=5_000_000, transcendentals=500_000
        ),
    )(
        hist_len, queries, gain_mix, gain_out,
        history_keys, cached_history_values, w_up, w_down,
    )
    return out.reshape(REQ_DEV, 1, WIDTH)


def solution(mesh):
    return jax.shard_map(
        local,
        mesh=mesh,
        in_specs=(
            P(),
            P(None, "token"),
            P(("batch", "hidden"), "token", None),
            P(("batch", "hidden"), "token", None),
            P(),
            P("token", None, "hidden"),
            P("token", "hidden", None),
            P(),
        ),
        out_specs=P(("batch", "hidden"), "token", None),
        check_vma=False,
    )
```
